512 devices in a mesh: row: 16 (over y, core), col: 32 (over z, x).
Axes of the slice: x: 4, y: 8, z: 8, core: 2. Of those that a mesh axis runs over, the one named last changes fastest.
Arguments:
- grad_out: bfloat16 [1024, 8192], P('col', 'row'), may hold values from -4 to 4
- saved_input: bfloat16 [1024, 53248], P('row', 'col'), may hold values from -2 to 2
- codes: bfloat16 [8192, 53248], P('row', 'col'), may hold values from -127 to 127, as said below
- exponents: int32 [8192], P('row'), may hold values from -14 to -11
Outputs:
- input_grad: bfloat16 [1024, 53248], P('row', 'col')
- weight_grad: bfloat16 [8192, 53248], P('row', 'col')
The draws below stay inside these ranges and needn't reach their ends.
Inputs may be any that keep to these rules, and one draw needn't show every extreme that they name: `codes`: every entry is a whole number.
All inputs are finite; a program needn't handle non-finite values.
Results may differ from the reference program's by a relative error of at most 0.001.
Values may be sent and summed in bfloat16 or wider, within the bound.
A program may use at most 64 MiB of HBM per device.

```python
import jax
import jax.numpy as jnp

D = 8192
FF = 53248
TOKENS = 1024


def draw_codes(key, part):
    key = jax.random.fold_in(key, 11)
    values = jax.random.randint(key, (D, FF), -127, 128, dtype=jnp.int32)
    return values.astype(jnp.float32).astype(jnp.bfloat16)


def with_ends(values, key, smallest, high):
    longest = values.shape.index(max(values.shape))
    spots = []
    for shift in (0, 1):
        where = [jax.random.randint(jax.random.fold_in(key, axis), (), 0, length) for axis, length in enumerate(values.shape)]
        where[longest] = (where[longest] + shift) % values.shape[longest]
        spots.append(tuple(where))
    return values.at[spots[0]].set(smallest).at[spots[1]].set(high)


def with_spikes(entries, rng, source, target, blocks, factor):
    owner, partner = [(jnp.arange(entries.shape[position]) // (entries.shape[position] // blocks)).reshape([-1 if axis == position else 1 for axis in range(entries.ndim)]) for position in (source, target)]
    chosen = jax.random.permutation(rng, blocks)[partner]
    strong = (owner == chosen) | (owner == (partner + blocks // 2) % blocks)
    return jnp.where(strong, factor * entries, entries)


def block_levels(own_key, shape, shards, least, largest):
    def one(dim, parts):
        steps = jax.random.uniform(jax.random.fold_in(jax.random.fold_in(own_key, 6), dim), (parts,), jnp.float32, least / len(shards), largest / len(shards))
        return jnp.repeat(jnp.exp(steps), shape[dim] // parts).reshape((-1,) + (1,) * (len(shape) - dim - 1))

    loudness = one(*shards[0])
    for cut in shards[1:]:
        loudness = loudness * one(*cut)
    return loudness


def normal_values(rng, shape, scale, bound, pieces=(), kind=jnp.bfloat16):
    result = scale * jax.random.normal(rng, shape, jnp.float32)
    if pieces:
        result = result * block_levels(rng, shape, pieces, -0.22, 0.18)
    return jnp.clip(result, -bound, bound).astype(kind)


def heavy_noise(stream_key, extent, width, limit, split, heavy, held_as=jnp.bfloat16):
    drawn = width * jax.random.normal(stream_key, extent, jnp.float32)
    if split:
        drawn = drawn * block_levels(stream_key, extent, split, -0.22, 0.18)
    return jnp.clip(with_spikes(drawn, jax.random.fold_in(stream_key, 3), *heavy), -limit, limit).astype(held_as)


def setup_inputs(seed: int = 0) -> dict:
    streams_of = jax.random.split(jax.random.key(seed), 5)
    return {
        "grad_out": heavy_noise(streams_of[0], (TOKENS, D), 0.5, 4.0, ((0, 32), (1, 16)), (1, 0, 32, 2.75)),
        "saved_input": normal_values(streams_of[1], (TOKENS, FF), 0.25, 2.0, ((0, 16), (1, 32))),
        "codes": draw_codes(jax.random.fold_in(streams_of[4], 71), 0),
        "exponents": with_ends(jax.random.randint(streams_of[3], (D,), -14, -10), jax.random.fold_in(streams_of[3], 1), -14, (-10) - 1).astype(jnp.int32),
    }


def reference(grad_out, saved_input, codes, exponents):
    scales = jnp.exp2(exponents.astype(jnp.float32))
    weight = (codes.astype(jnp.float32) * scales[:, None]).astype(jnp.bfloat16)
    input_grad = jnp.dot(grad_out, weight, preferred_element_type=jnp.float32).astype(jnp.bfloat16)
    weight_grad = jnp.dot(grad_out.T, saved_input, preferred_element_type=jnp.float32).astype(jnp.bfloat16)
    return input_grad, weight_grad
```

```python
import functools

import jax
import jax.numpy as jnp
from jax import lax
from jax.experimental import pallas as pl
from jax.experimental.pallas import tpu as pltpu
from jax.sharding import PartitionSpec as P

MESH = pl.DeviceIdType.MESH
NY, NZ, NX = 8, 8, 4
CH, FB, TB = 512, 1664, 64
LANES = FB // 128
TOP = 32700.0
COPIES = 80
PARTS = ("go", "si", "mm", "rs")


def encode(value, out):
    top = jnp.max(jnp.max(jnp.abs(value), axis=0), axis=1, keepdims=True)
    code = jnp.ceil(16.0 * jnp.log2(jnp.maximum(top, 1e-30)))
    scale = jnp.exp2(code * (-1.0 / 16)) * TOP
    out[...] = jnp.round(value * scale[None]).astype(jnp.int32).astype(jnp.int16)
    return code


def kernel(g_in, s_in, c_in, e_in, ig_out, wg_out, S, G, W, A, T, GT, Q, WG, IG, TX, RX, lsem, ssem, rsem):
    row, col = lax.axis_index("row"), lax.axis_index("col")
    y, core = lax.div(row, 2), lax.rem(row, 2)
    z, x = lax.div(col, NX), lax.rem(col, NX)
    sent = []

    def device(dy=0, dz=0, dx=0, other=False):
        yy = lax.rem(y + dy + NY, NY)
        cc = 1 - core if other else core
        return (yy * 2 + cc, lax.rem(z + dz + NZ, NZ) * NX + lax.rem(x + dx + NX, NX))

    def send(src, dst, to):
        k = len(sent)
        copy = pltpu.make_async_remote_copy(
            src_ref=src, dst_ref=dst, send_sem=ssem.at[k], recv_sem=rsem.at[k], device_id=to, device_id_type=MESH
        )
        copy.start()
        sent.append(copy)
        return copy

    def local(src, dst, k):
        copy = pltpu.make_async_copy(src, dst, lsem.at[k])
        copy.start()
        return copy

    sibling = device(other=True)
    y_to = {1: device(dy=1), -1: device(dy=-1)}
    z_to = {1: device(dz=1), -1: device(dz=-1)}
    x_to = [device(dx=d) for d in (1, 2, 3)]

    barrier = pltpu.get_barrier_semaphore()
    partners = [sibling, *y_to.values(), *z_to.values(), *x_to]
    for partner in partners:
        pl.semaphore_signal(barrier, inc=1, device_id=partner, device_id_type=MESH)
    pl.semaphore_wait(barrier, len(partners))

    def y_at(d):
        return lax.rem(y + d + 2 * NY, NY)

    def z_at(d):
        return lax.rem(z + d + 2 * NZ, NZ)

    go, si, mm, rs = (p in PARTS for p in ("go", "si", "mm", "rs"))

    mine = pl.ds(pl.multiple_of(lax.rem(x, 2) * 32, 32), 32)
    if go:
        own_g = local(g_in, G.at[z, lax.div(x, 2), mine], 0)
        g_x = [send(g_in, G.at[z, lax.div(x, 2), mine], to) for to in x_to]
    if si:
        s_y = {}
        for h in (0, 1):
            for d in (1, -1):
                s_y[d, h, 0] = send(s_in.at[h], S.at[y * 2 + core, h], y_to[d])
        s_sib = [send(s_in, S.at[y * 2 + core], sibling)]
        own_s = local(s_in, S.at[y * 2 + core], 1)
    if mm:
        codes = send(c_in, W.at[1], sibling)
        own_c = local(c_in, W.at[0], 2)

    def forward_s(step):
        for h in (0, 1):
            for d in (1, -1):
                if (d, h, step) in s_y:
                    s_y[d, h, step].wait_recv()
                    block = S.at[y_at(-d * (step + 1)) * 2 + core, h]
                    if step < 2 or (step == 2 and h == (0 if d == 1 else 1)):
                        s_y[d, h, step + 1] = send(block, block, y_to[d])
                    s_sib.append(send(block, block, sibling))

    g_z = {}

    def forward_g(step):
        for h in (0, 1):
            for d in (1, -1):
                if step == 0:
                    slab = G.at[z, h]
                else:
                    g_z[d, h, step - 1].wait_recv()
                    slab = G.at[z_at(-d * step), h]
                if step < 3 or (step == 3 and h == (0 if d == 1 else 1)):
                    g_z[d, h, step] = send(slab, slab, z_to[d])

    if go:
        own_g.wait()
        for copy in g_x:
            copy.wait_recv()
        forward_g(0)
        if si:
            forward_s(0)
        forward_g(1)
        if si:
            forward_s(1)
        forward_g(2)
        forward_g(3)
        g_z[1, 0, 3].wait_recv()
        g_z[-1, 1, 3].wait_recv()
    elif si:
        forward_s(0)
        forward_s(1)

    if mm:
        scale = jnp.exp2((e_in[...] + 14).astype(jnp.float32)).astype(jnp.bfloat16).reshape(1, 1, CH)
        T[...] = G[:, 1 - core] * scale
        act = send(T, A.at[1], sibling)
        A[0] = G[:, core] * scale
        GT[...] = G[...].reshape(NZ * 128, CH).T
    if si:
        forward_s(2)
    if mm:
        own_c.wait()
        codes.wait_recv()
        act.wait_recv()

        def tile_of_q(at, width):
            cols = pl.ds(at, width)
            tile = jnp.dot(A[0].reshape(NY * TB, CH), W[0, :, cols], preferred_element_type=jnp.float32)
            tile += jnp.dot(A[1].reshape(NY * TB, CH), W[1, :, cols], preferred_element_type=jnp.float32)
            return tile

        @pl.loop(0, LANES // 2)
        def _(j):
            tile = tile_of_q(pl.multiple_of(j * 256, 256), 256)
            for i in (0, 1):
                Q[:, :, j * 2 + i] = tile[:, i * 128 : i * 128 + 128].reshape(NY, 4, 16, 128)

        Q[:, :, LANES - 1] = tile_of_q(128 * (LANES - 1), 128).reshape(NY, 4, 16, 128)

    def tile_of_wg(at, width):
        cols = pl.ds(at, width)
        tile = jnp.dot(GT[...], S[:, :, :, cols].reshape(1024, width), preferred_element_type=jnp.float32)
        WG[:, cols] = tile.astype(jnp.bfloat16)

    def wgrad(part):
        if part == 0:
            own_s.wait()
            for copy in s_sib:
                copy.wait_recv()

        @pl.loop(part * 2, part * 2 + 2)
        def _(j):
            tile_of_wg(pl.multiple_of(j * 256, 256), 256)

        if part == 2:
            tile_of_wg(128 * (LANES - 1), 128)
            return local(WG, wg_out, 3)

    half_lane = lax.broadcasted_iota(jnp.int32, (16, 128), 1) < 64

    def scales(message):
        tile = jnp.exp2(message[2 * LANES].astype(jnp.int32).astype(jnp.float32) * (1.0 / 16)) * (1.0 / TOP)
        turned = pltpu.roll(tile, 64, 1)
        return jnp.where(half_lane, tile, turned), jnp.where(half_lane, turned, tile)

    def decoded(message, group, scale):
        return message[pl.ds(LANES * group, LANES)].astype(jnp.int32).astype(jnp.float32) * scale[None]

    sums = {}

    def reduce_step(step):
        for h in (0, 1):
            for d in (1, -1):
                starts = 0 if h == (0 if d == 1 else 1) else 1
                if step < starts:
                    continue
                to = y_at(d * (4 - step))
                k = 0 if d == 1 else 1
                if step > starts:
                    sums[d, h, step - 1].wait_recv()
                    scale = scales(RX.at[k, h, step - 1])
                codes = []
                for g in (0, 1):
                    value = Q[to, 2 * h + g]
                    if step > starts:
                        value += decoded(RX.at[k, h, step - 1], g, scale[g])
                    codes.append(encode(value, TX.at[k, h, step, pl.ds(LANES * g, LANES)]))
                TX[k, h, step, 2 * LANES] = jnp.where(half_lane, codes[0], codes[1]).astype(jnp.int32).astype(jnp.int16)
                sums[d, h, step] = send(TX.at[k, h, step], RX.at[k, h, step], y_to[d])

    def finish():
        for h in (0, 1):
            for k, d in ((0, 1), (1, -1)):
                sums[d, h, 3].wait_recv()
            scale = [scales(RX.at[k, h, 3]) for k in (0, 1)]
            for g in (0, 1):
                value = Q[y, 2 * h + g]
                for k in (0, 1):
                    value += decoded(RX.at[k, h, 3], g, scale[k][g])
                value = (value * 2.0**-14).astype(jnp.bfloat16)
                for j in range(LANES):
                    IG[pl.ds(32 * h + 16 * g, 16), pl.ds(128 * j, 128)] = value[j]
        return local(IG, ig_out, 4)

    ends = []
    if rs:
        reduce_step(0)
        reduce_step(1)
    if si:
        s_y[1, 0, 3].wait_recv()
        s_y[-1, 1, 3].wait_recv()
        for d, h in ((1, 0), (-1, 1)):
            block = S.at[y_at(4) * 2 + core, h]
            s_sib.append(send(block, block, sibling))
    if mm and si:
        wgrad(0)
    if rs:
        reduce_step(2)
    if mm and si:
        wgrad(1)
    if rs:
        reduce_step(3)
    if mm and si:
        ends.append(wgrad(2))
    if rs:
        ends.append(finish())
    for copy in ends:
        copy.wait()
    for copy in sent:
        copy.wait_send()
    if not mm:
        if si:
            own_s.wait()
            for copy in s_sib:
                copy.wait_recv()
    if mm and not rs:
        pass


def local_part(grad_out, saved_input, codes, exponents):
    any_ = pl.BlockSpec(memory_space=pl.ANY)
    bf16 = jnp.bfloat16
    return pl.pallas_call(
        kernel,
        out_shape=(jax.ShapeDtypeStruct((TB, FB), bf16), jax.ShapeDtypeStruct((CH, FB), bf16)),
        in_specs=[any_, any_, any_, pl.BlockSpec(memory_space=pltpu.VMEM)],
        out_specs=(any_, any_),
        scratch_shapes=[
            pltpu.VMEM((2 * NY, 2, 32, FB), bf16),
            pltpu.VMEM((NZ, 2, TB, CH), bf16),
            pltpu.VMEM((2, CH, FB), bf16),
            pltpu.VMEM((2, NY, TB, CH), bf16),
            pltpu.VMEM((NY, TB, CH), bf16),
            pltpu.VMEM((CH, 2 * NY * TB), bf16),
            pltpu.VMEM((NY, 4, LANES, 16, 128), jnp.float32),
            pltpu.VMEM((CH, FB), bf16),
            pltpu.VMEM((TB, FB), bf16),
            pltpu.VMEM((2, 2, 4, 2 * LANES + 1, 16, 128), jnp.int16),
            pltpu.VMEM((2, 2, 4, 2 * LANES + 1, 16, 128), jnp.int16),
            pltpu.SemaphoreType.DMA((5,)),
            pltpu.SemaphoreType.DMA((COPIES,)),
            pltpu.SemaphoreType.DMA((COPIES,)),
        ],
        compiler_params=pltpu.CompilerParams(collective_id=0, has_side_effects=True, vmem_limit_bytes=48 * 1024 * 1024),
        cost_estimate=pl.CostEstimate(flops=4 * 1024 * CH * FB, bytes_accessed=8_000_000, transcendentals=0),
    )(grad_out, saved_input.reshape(2, 32, FB), codes, exponents)


def solution(mesh):
    in_specs = (P("col", "row"), P("row", "col"), P("row", "col"), P("row"))
    out_specs = (P("row", "col"), P("row", "col"))
    return jax.shard_map(local_part, mesh=mesh, in_specs=in_specs, out_specs=out_specs, check_vma=False)
```

```python
import jax
import jax.numpy as jnp
from jax import lax
from jax.experimental import pallas as pl
from jax.experimental.pallas import tpu as pltpu
from jax.sharding import PartitionSpec as P

MESH = pl.DeviceIdType.MESH
NY, NZ, NX = 8, 8, 4
CH, FB, TB = 512, 1664, 64
LANES = FB // 128
TOP = 32700.0
COPIES = 112
ZX = 384
ORDER = (4, 3, -3, 2, -2, 1, -1, 0)
VMEM_LIMIT = 52 * 1000 * 1024


def encode(value, out):
    top = jnp.max(jnp.max(jnp.abs(value), axis=0), axis=1, keepdims=True)
    code = jnp.ceil(16.0 * jnp.log2(jnp.maximum(top, 1e-30)))
    scale = jnp.exp2(code * (-1.0 / 16)) * TOP
    out[pl.ds(0, LANES)] = jnp.round(value * scale[None]).astype(jnp.int32).astype(jnp.int16)
    out[LANES] = jnp.broadcast_to(code, (16, 128)).astype(jnp.int32).astype(jnp.int16)


def decode(message):
    scale = jnp.exp2(message[LANES].astype(jnp.int32).astype(jnp.float32) * (1.0 / 16)) * (1.0 / TOP)
    return message[pl.ds(0, LANES)].astype(jnp.int32).astype(jnp.float32) * scale[None]


def kernel(g_in, s_in, c_in, e_in, ig_out, wg_out, S, G, W, E, A, T, GT, Q, WG, IG, TX, RX, lsem, ssem, rsem):
    row, col = lax.axis_index("row"), lax.axis_index("col")
    y, core = lax.div(row, 2), lax.rem(row, 2)
    z, x = lax.div(col, NX), lax.rem(col, NX)
    sent = []

    def device(dy=0, dz=0, dx=0, other=False):
        yy = lax.rem(y + dy + NY, NY)
        cc = 1 - core if other else core
        return (yy * 2 + cc, lax.rem(z + dz + NZ, NZ) * NX + lax.rem(x + dx + NX, NX))

    def send(src, dst, to):
        k = len(sent)
        copy = pltpu.make_async_remote_copy(
            src_ref=src, dst_ref=dst, send_sem=ssem.at[k], recv_sem=rsem.at[k], device_id=to, device_id_type=MESH
        )
        copy.start()
        sent.append(copy)
        return copy

    def local(src, dst, k):
        copy = pltpu.make_async_copy(src, dst, lsem.at[k])
        copy.start()
        return copy

    sibling = device(other=True)
    y_to = {d: device(dy=d) for d in (1, -1)}
    z_to = {d: device(dz=d) for d in (1, -1, 2, -2, 3, -3, 4)}
    x_to = {d: device(dx=d) for d in (2, 1, -1)}

    own_g = local(g_in, G.at[z, x], 0)
    own_s = local(s_in, S.at[y * 2 + core], 1)
    own_c = local(c_in, W.at[0], 2)
    own_e = local(e_in, E, 3)

    barrier = pltpu.get_barrier_semaphore()
    partners = [sibling, *y_to.values(), *z_to.values(), *x_to.values()]
    for partner in partners:
        pl.semaphore_signal(barrier, inc=1, device_id=partner, device_id_type=MESH)
    pl.semaphore_wait(barrier, len(partners))

    def y_at(d):
        return lax.rem(y + d + 2 * NY, NY)

    def z_at(d):
        return lax.rem(z + d + 2 * NZ, NZ)

    zx, xz = pl.ds(0, ZX), pl.ds(ZX, CH - ZX)
    h_x = {d: send(g_in.at[:, xz], G.at[z, x, :, xz], to) for d, to in x_to.items()}
    g_z = {d: send(g_in.at[:, zx], G.at[z, x, :, zx], to) for d, to in z_to.items()}
    g_x = {(d, 0): send(g_in.at[:, zx], G.at[z, x, :, zx], to) for d, to in x_to.items()}
    s_y = {}
    for h in (0, 1):
        for d in (1, -1):
            s_y[d, h, 0] = send(s_in.at[h], S.at[y * 2 + core, h], y_to[d])
    s_sib = [send(s_in, S.at[y * 2 + core], sibling)]
    codes = send(c_in, W.at[1], sibling)

    def forward_g(d):
        g_z[d].wait_recv()
        chunk = G.at[z_at(-d), x, :, zx]
        for dx, to in x_to.items():
            g_x[dx, d] = send(chunk, chunk, to)

    def forward_s(step, h):
        for d in (1, -1):
            if (d, h, step) in s_y:
                s_y[d, h, step].wait_recv()
                block = S.at[y_at(-d * (step + 1)) * 2 + core, h]
                if step < 2 or (step == 2 and h == (0 if d == 1 else 1)):
                    s_y[d, h, step + 1] = send(block, block, y_to[d])
                s_sib.append(send(block, block, sibling))

    own_g.wait()
    for d in x_to:
        h_x[d].wait_recv()
    h_z = {d: send(G.at[z, :, :, xz], G.at[z, :, :, xz], to) for d, to in z_to.items()}
    for d in (1, -1, 2, -2):
        forward_g(d)
    forward_s(0, 0)
    for d in (3, -3):
        forward_g(d)
    forward_s(0, 1)
    forward_g(4)
    for d in (0, 1, -1, 2, -2, 3, -3):
        for dx in x_to:
            g_x[dx, d].wait_recv()
    forward_s(1, 0)
    forward_s(1, 1)
    for dx in x_to:
        g_x[dx, 4].wait_recv()
    for d in z_to:
        h_z[d].wait_recv()
    own_e.wait()

    scale = jnp.exp2((E[...] + 14).astype(jnp.float32)).astype(jnp.bfloat16).reshape(1, 1, CH)

    def scaled(slots, part, out):
        for k in slots:
            block = G[y_at(ORDER[k]), pl.ds(2 * part, 2)] * scale
            out[k] = block.reshape(TB, CH)

    first, second = range(0, 3), range(3, NY)
    acts = []
    for slots in (first, second):
        at = pl.ds(slots[0], len(slots))
        scaled(slots, 1 - core, T)
        acts.append(send(T.at[at], A.at[1, at], sibling))
    scaled(range(NY), core, A.at[0])
    own_c.wait()
    codes.wait_recv()

    def matmul(slots):
        at, rows = pl.ds(slots[0], len(slots)), len(slots) * TB

        def tile(cols):
            return sum(
                jnp.dot(A[i, at].reshape(rows, CH), W[i, :, cols], preferred_element_type=jnp.float32) for i in (0, 1)
            )

        @pl.loop(0, LANES // 2)
        def _(j):
            value = tile(pl.ds(pl.multiple_of(j * 256, 256), 256))
            for i in (0, 1):
                Q[at, :, j * 2 + i] = value[:, i * 128 : i * 128 + 128].reshape(len(slots), 4, 16, 128)

        Q[at, :, LANES - 1] = tile(pl.ds(128 * (LANES - 1), 128)).reshape(len(slots), 4, 16, 128)

    sums = {}

    def chains(step, longer):
        starts = 0 if longer else 1
        for g in (0, 1):
            for k, d in enumerate((1, -1)):
                h = k if longer else 1 - k
                value = Q[ORDER.index(d * (4 - step) if step else 4), 2 * h + g]
                if step > starts:
                    sums[k, h, g, step - 1].wait_recv()
                    value += decode(RX.at[k, h, g, step - 1])
                out = TX.at[k, h, g, step]
                encode(value, out)
                sums[k, h, g, step] = send(out, RX.at[k, h, g, step], y_to[d])

    def finish():
        for h in (0, 1):
            for g in (0, 1):
                value = Q[NY - 1, 2 * h + g]
                for k in (0, 1):
                    sums[k, h, g, 3].wait_recv()
                    value += decode(RX.at[k, h, g, 3])
                value = (value * 2.0**-14).astype(jnp.bfloat16)
                for j in range(LANES):
                    IG[pl.ds(32 * h + 16 * g, 16), pl.ds(128 * j, 128)] = value[j]
        return local(IG, ig_out, 4)

    def wgrad():
        def tile(cols, width):
            value = jnp.dot(GT[...], S[:, :, :, cols].reshape(1024, width), preferred_element_type=jnp.float32)
            WG[:, cols] = value.astype(jnp.bfloat16)

        @pl.loop(0, LANES // 2)
        def _(j):
            tile(pl.ds(pl.multiple_of(j * 256, 256), 256), 256)

        tile(pl.ds(128 * (LANES - 1), 128), 128)
        return local(WG, wg_out, 5)

    acts[0].wait_recv()
    matmul(first)
    chains(0, True)
    chains(1, False)
    acts[1].wait_recv()
    matmul(second)
    GT[...] = G[...].reshape(1024, CH).T
    chains(1, True)
    forward_s(2, 0)
    chains(2, False)
    forward_s(2, 1)
    chains(2, True)
    forward_s(3, 0)
    forward_s(3, 1)
    chains(3, False)
    chains(3, True)
    own_s.wait()
    for copy in s_sib:
        copy.wait_recv()
    ends = [wgrad(), finish()]
    for copy in ends:
        copy.wait()
    for copy in sent:
        copy.wait_send()


def local_part(grad_out, saved_input, codes, exponents):
    any_, hbm = pl.BlockSpec(memory_space=pl.ANY), pl.BlockSpec(memory_space=pltpu.HBM)
    bf16 = jnp.bfloat16
    message = (2, 2, 2, 4, LANES + 1, 16, 128)
    return pl.pallas_call(
        kernel,
        out_shape=(jax.ShapeDtypeStruct((TB, FB), bf16), jax.ShapeDtypeStruct((CH, FB), bf16)),
        in_specs=[hbm, hbm, hbm, hbm],
        out_specs=(any_, any_),
        scratch_shapes=[
            pltpu.VMEM((2 * NY, 2, 32, FB), bf16),
            pltpu.VMEM((NZ, NX, 32, CH), bf16),
            pltpu.VMEM((2, CH, FB), bf16),
            pltpu.VMEM((CH,), jnp.int32),
            pltpu.VMEM((2, NY, TB, CH), bf16),
            pltpu.VMEM((NY, TB, CH), bf16),
            pltpu.VMEM((CH, 2 * NY * TB), bf16),
            pltpu.VMEM((NY, 4, LANES, 16, 128), jnp.float32),
            pltpu.VMEM((CH, FB), bf16),
            pltpu.VMEM((TB, FB), bf16),
            pltpu.VMEM(message, jnp.int16),
            pltpu.VMEM(message, jnp.int16),
            pltpu.SemaphoreType.DMA((6,)),
            pltpu.SemaphoreType.DMA((COPIES,)),
            pltpu.SemaphoreType.DMA((COPIES,)),
        ],
        compiler_params=pltpu.CompilerParams(collective_id=0, has_side_effects=True, vmem_limit_bytes=VMEM_LIMIT),
        cost_estimate=pl.CostEstimate(flops=4 * 1024 * CH * FB, bytes_accessed=8_000_000, transcendentals=0),
    )(*(pltpu.with_memory_space_constraint(a, pltpu.HBM) for a in (grad_out, saved_input.reshape(2, 32, FB), codes, exponents)))


def solution(mesh):
    in_specs = (P("col", "row"), P("row", "col"), P("row", "col"), P("row"))
    out_specs = (P("row", "col"), P("row", "col"))
    return jax.shard_map(local_part, mesh=mesh, in_specs=in_specs, out_specs=out_specs, check_vma=False)
```

```python
import jax
import jax.numpy as jnp
from jax import lax
from jax.experimental import pallas as pl
from jax.experimental.pallas import tpu as pltpu
from jax.sharding import PartitionSpec as P

MESH = pl.DeviceIdType.MESH
NY, NZ, NX = 8, 8, 4
CH, FB, TB = 512, 1664, 64
LANES = FB // 128
TOP = 32700.0
COPIES = 112
ZX = 384
ORDER = (4, 3, -3, 2, -2, 1, -1, 0)
VMEM_LIMIT = 52 * 1000 * 1024


def encode(value, out):
    top = jnp.max(jnp.max(jnp.abs(value), axis=0), axis=1, keepdims=True)
    code = jnp.ceil(16.0 * jnp.log2(jnp.maximum(top, 1e-30)))
    scale = jnp.exp2(code * (-1.0 / 16)) * TOP
    out[pl.ds(0, LANES)] = jnp.round(value * scale[None]).astype(jnp.int32).astype(jnp.int16)
    out[LANES] = jnp.broadcast_to(code, (16, 128)).astype(jnp.int32).astype(jnp.int16)


def decode(message):
    scale = jnp.exp2(message[LANES].astype(jnp.int32).astype(jnp.float32) * (1.0 / 16)) * (1.0 / TOP)
    return message[pl.ds(0, LANES)].astype(jnp.int32).astype(jnp.float32) * scale[None]


def kernel(g_in, s_in, c_in, e_in, ig_out, wg_out, S, G, W, E, A, T, GT, Q, WG, IG, TX, RX, lsem, ssem, rsem):
    row, col = lax.axis_index("row"), lax.axis_index("col")
    y, core = lax.div(row, 2), lax.rem(row, 2)
    z, x = lax.div(col, NX), lax.rem(col, NX)
    sent = []

    def device(dy=0, dz=0, dx=0, other=False):
        yy = lax.rem(y + dy + NY, NY)
        cc = 1 - core if other else core
        return (yy * 2 + cc, lax.rem(z + dz + NZ, NZ) * NX + lax.rem(x + dx + NX, NX))

    def send(src, dst, to):
        k = len(sent)
        copy = pltpu.make_async_remote_copy(
            src_ref=src, dst_ref=dst, send_sem=ssem.at[k], recv_sem=rsem.at[k], device_id=to, device_id_type=MESH
        )
        copy.start()
        sent.append(copy)
        return copy

    def local(src, dst, k):
        copy = pltpu.make_async_copy(src, dst, lsem.at[k])
        copy.start()
        return copy

    sibling = device(other=True)
    y_to = {d: device(dy=d) for d in (1, -1)}
    z_to = {d: device(dz=d) for d in (1, -1, 2, -2, 3, -3, 4)}
    x_to = {d: device(dx=d) for d in (2, 1, -1)}

    own_g = local(g_in, G.at[z, x], 0)
    own_s = local(s_in, S.at[y * 2 + core], 1)
    own_c = local(c_in, W.at[0], 2)
    own_e = local(e_in, E, 3)

    barrier = pltpu.get_barrier_semaphore()
    partners = [sibling, *y_to.values(), *z_to.values(), *x_to.values()]
    for partner in partners:
        pl.semaphore_signal(barrier, inc=1, device_id=partner, device_id_type=MESH)
    pl.semaphore_wait(barrier, len(partners))

    def y_at(d):
        return lax.rem(y + d + 2 * NY, NY)

    def z_at(d):
        return lax.rem(z + d + 2 * NZ, NZ)

    def far_half(d, far):
        return 0 if (d == 1) == far else 1

    zx, xz = pl.ds(0, ZX), pl.ds(ZX, CH - ZX)
    h_x = {d: send(g_in.at[:, xz], G.at[z, x, :, xz], to) for d, to in x_to.items()}
    g_z = {d: send(g_in.at[:, zx], G.at[z, x, :, zx], to) for d, to in z_to.items()}
    g_x = {(d, 0): send(g_in.at[:, zx], G.at[z, x, :, zx], to) for d, to in x_to.items()}
    s_y = {}
    for far in (True, False):
        for d in (1, -1):
            h = far_half(d, far)
            s_y[d, h, 0] = send(s_in.at[h], S.at[y * 2 + core, h], y_to[d])
    s_sib = [send(s_in, S.at[y * 2 + core], sibling)]
    codes = send(c_in, W.at[1], sibling)

    def forward_g(d):
        g_z[d].wait_recv()
        chunk = G.at[z_at(-d), x, :, zx]
        for dx, to in x_to.items():
            g_x[dx, d] = send(chunk, chunk, to)

    def forward_s(step, far):
        for d in (1, -1):
            h = far_half(d, far)
            s_y[d, h, step].wait_recv()
            block = S.at[y_at(-d * (step + 1)) * 2 + core, h]
            if step < (3 if far else 2):
                s_y[d, h, step + 1] = send(block, block, y_to[d])
            s_sib.append(send(block, block, sibling))

    own_e.wait()
    scale = jnp.exp2((E[...] + 14).astype(jnp.float32)).astype(jnp.bfloat16).reshape(1, 1, CH)
    own_g.wait()
    for d in x_to:
        h_x[d].wait_recv()
    h_z = {d: send(G.at[z, :, :, xz], G.at[z, :, :, xz], to) for d, to in z_to.items()}
    for d in (1, -1, 2, -2):
        forward_g(d)
    forward_s(0, True)
    for d in (3, -3):
        forward_g(d)
    forward_s(0, False)
    forward_g(4)

    def arrived(d):
        for dx in x_to:
            g_x[dx, d].wait_recv()
        if d:
            h_z[d].wait_recv()

    for d in (0, 1, -1, 2, -2):
        arrived(d)
    forward_s(1, True)
    for d in (3, -3):
        arrived(d)
    forward_s(1, False)
    arrived(4)
    def scaled(slots, part, out):
        for k in slots:
            block = G[y_at(ORDER[k]), pl.ds(2 * part, 2)] * scale
            out[k] = block.reshape(TB, CH)

    first, second = range(0, 3), range(3, NY)
    acts = {}

    def exchange(slots):
        at = pl.ds(slots[0], len(slots))
        scaled(slots, 1 - core, T)
        acts[slots] = send(T.at[at], A.at[1, at], sibling)
        scaled(slots, core, A.at[0])

    def matmul(slots):
        at, rows = pl.ds(slots[0], len(slots)), len(slots) * TB

        def tile(cols):
            return sum(
                jnp.dot(A[i, at].reshape(rows, CH), W[i, :, cols], preferred_element_type=jnp.float32) for i in (0, 1)
            )

        @pl.loop(0, LANES // 2)
        def _(j):
            value = tile(pl.ds(pl.multiple_of(j * 256, 256), 256))
            for i in (0, 1):
                Q[at, :, j * 2 + i] = value[:, i * 128 : i * 128 + 128].reshape(len(slots), 4, 16, 128)

        Q[at, :, LANES - 1] = tile(pl.ds(128 * (LANES - 1), 128)).reshape(len(slots), 4, 16, 128)

    sums = {}

    def chains(step, longer):
        starts = 0 if longer else 1
        for g in (0, 1):
            for k, d in enumerate((1, -1)):
                h = k if longer else 1 - k
                value = Q[ORDER.index(d * (4 - step) if step else 4), 2 * h + g]
                if step > starts:
                    sums[k, h, g, step - 1].wait_recv()
                    value += decode(RX.at[k, h, g, step - 1])
                out = TX.at[k, h, g, step]
                encode(value, out)
                sums[k, h, g, step] = send(out, RX.at[k, h, g, step], y_to[d])

    def finish():
        for h in (0, 1):
            for g in (0, 1):
                value = Q[NY - 1, 2 * h + g]
                for k in (0, 1):
                    sums[k, h, g, 3].wait_recv()
                    value += decode(RX.at[k, h, g, 3])
                value = (value * 2.0**-14).astype(jnp.bfloat16)
                for j in range(LANES):
                    IG[pl.ds(32 * h + 16 * g, 16), pl.ds(128 * j, 128)] = value[j]
        return local(IG, ig_out, 4)

    def wgrad():
        def tile(cols, width):
            value = jnp.dot(GT[...], S[:, :, :, cols].reshape(1024, width), preferred_element_type=jnp.float32)
            WG[:, cols] = value.astype(jnp.bfloat16)

        @pl.loop(0, LANES // 2)
        def _(j):
            tile(pl.ds(pl.multiple_of(j * 256, 256), 256), 256)

        tile(pl.ds(128 * (LANES - 1), 128), 128)
        return local(WG, wg_out, 5)

    exchange(first)
    own_c.wait()
    codes.wait_recv()
    acts[first].wait_recv()
    matmul(first)
    chains(0, True)
    chains(1, False)
    exchange(second)
    forward_s(2, True)
    acts[second].wait_recv()
    matmul(second)
    chains(1, True)
    GT[...] = G[...].reshape(1024, CH).T
    chains(2, False)
    forward_s(2, False)
    chains(2, True)
    chains(3, False)
    chains(3, True)
    forward_s(3, True)
    own_s.wait()
    for copy in s_sib:
        copy.wait_recv()
    ends = [wgrad(), finish()]
    for copy in ends:
        copy.wait()
    for copy in sent:
        copy.wait_send()


def store(ig_in, wg_in, ig_out, wg_out, sem):
    copies = [pltpu.make_async_copy(wg_in, wg_out, sem.at[0]), pltpu.make_async_copy(ig_in, ig_out, sem.at[1])]
    for copy in copies:
        copy.start()
    for copy in copies:
        copy.wait()


def local_part(grad_out, saved_input, codes, exponents):
    any_, hbm = pl.BlockSpec(memory_space=pl.ANY), pl.BlockSpec(memory_space=pltpu.HBM)
    bf16 = jnp.bfloat16
    message = (2, 2, 2, 4, LANES + 1, 16, 128)
    shapes = (jax.ShapeDtypeStruct((TB, FB), bf16), jax.ShapeDtypeStruct((CH, FB), bf16))
    grads = pl.pallas_call(
        kernel,
        out_shape=shapes,
        in_specs=[hbm, hbm, hbm, hbm],
        out_specs=(any_, any_),
        scratch_shapes=[
            pltpu.VMEM((2 * NY, 2, 32, FB), bf16),
            pltpu.VMEM((NZ, NX, 32, CH), bf16),
            pltpu.VMEM((2, CH, FB), bf16),
            pltpu.VMEM((CH,), jnp.int32),
            pltpu.VMEM((2, NY, TB, CH), bf16),
            pltpu.VMEM((NY, TB, CH), bf16),
            pltpu.VMEM((CH, 2 * NY * TB), bf16),
            pltpu.VMEM((NY, 4, LANES, 16, 128), jnp.float32),
            pltpu.VMEM((CH, FB), bf16),
            pltpu.VMEM((TB, FB), bf16),
            pltpu.VMEM(message, jnp.int16),
            pltpu.VMEM(message, jnp.int16),
            pltpu.SemaphoreType.DMA((6,)),
            pltpu.SemaphoreType.DMA((COPIES,)),
            pltpu.SemaphoreType.DMA((COPIES,)),
        ],
        compiler_params=pltpu.CompilerParams(collective_id=0, has_side_effects=True, vmem_limit_bytes=VMEM_LIMIT),
        cost_estimate=pl.CostEstimate(flops=4 * 1024 * CH * FB, bytes_accessed=8_000_000, transcendentals=0),
    )(*(pltpu.with_memory_space_constraint(a, pltpu.HBM) for a in (grad_out, saved_input.reshape(2, 32, FB), codes, exponents)))
    return pl.pallas_call(
        store,
        out_shape=shapes,
        in_specs=[any_, any_],
        out_specs=(any_, any_),
        scratch_shapes=[pltpu.SemaphoreType.DMA((2,))],
        compiler_params=pltpu.CompilerParams(vmem_limit_bytes=1024 * 1024),
    )(*grads)


def solution(mesh):
    in_specs = (P("col", "row"), P("row", "col"), P("row", "col"), P("row"))
    out_specs = (P("row", "col"), P("row", "col"))
    return jax.shard_map(local_part, mesh=mesh, in_specs=in_specs, out_specs=out_specs, check_vma=False)
```

```python
import jax
import jax.numpy as jnp
from jax import lax
from jax.experimental import pallas as pl
from jax.experimental.pallas import tpu as pltpu
from jax.sharding import PartitionSpec as P

MESH = pl.DeviceIdType.MESH
NY, NZ, NX = 8, 8, 4
CH, FB, TB = 512, 1664, 64
LANES = FB // 128
TOP = 32700.0
COPIES = 112
ZX = 384
ORDER = (4, 3, -3, 2, -2, 1, -1, 0)
VMEM_LIMIT = 52 * 1000 * 1024


def encode(value, out):
    top = jnp.max(jnp.max(jnp.abs(value), axis=0), axis=1, keepdims=True)
    code = jnp.ceil(16.0 * jnp.log2(jnp.maximum(top, 1e-30)))
    scale = jnp.exp2(code * (-1.0 / 16)) * TOP
    out[pl.ds(0, LANES)] = jnp.round(value * scale[None]).astype(jnp.int32).astype(jnp.int16)
    out[LANES] = jnp.broadcast_to(code, (16, 128)).astype(jnp.int32).astype(jnp.int16)


def decode(message):
    scale = jnp.exp2(message[LANES].astype(jnp.int32).astype(jnp.float32) * (1.0 / 16)) * (1.0 / TOP)
    return message[pl.ds(0, LANES)].astype(jnp.int32).astype(jnp.float32) * scale[None]


def kernel(g_in, s_in, c_in, e_in, ig_out, wg_out, S, G, W, E, A, T, GT, Q, WG, TX, RX, lsem, ssem, rsem):
    row, col = lax.axis_index("row"), lax.axis_index("col")
    y, core = lax.div(row, 2), lax.rem(row, 2)
    z, x = lax.div(col, NX), lax.rem(col, NX)
    sent = []

    def device(dy=0, dz=0, dx=0, other=False):
        yy = lax.rem(y + dy + NY, NY)
        cc = 1 - core if other else core
        return (yy * 2 + cc, lax.rem(z + dz + NZ, NZ) * NX + lax.rem(x + dx + NX, NX))

    def send(src, dst, to):
        k = len(sent)
        copy = pltpu.make_async_remote_copy(
            src_ref=src, dst_ref=dst, send_sem=ssem.at[k], recv_sem=rsem.at[k], device_id=to, device_id_type=MESH
        )
        copy.start()
        sent.append(copy)
        return copy

    def local(src, dst, k):
        copy = pltpu.make_async_copy(src, dst, lsem.at[k])
        copy.start()
        return copy

    sibling = device(other=True)
    y_to = {d: device(dy=d) for d in (1, -1)}
    z_to = {d: device(dz=d) for d in (1, -1, 2, -2, 3, -3, 4)}
    x_to = {d: device(dx=d) for d in (2, 1, -1)}

    own_g = local(g_in, G.at[z, x], 0)
    own_s = local(s_in, S.at[y * 2 + core], 1)
    own_c = local(c_in, W.at[0], 2)
    own_e = local(e_in, E, 3)

    barrier = pltpu.get_barrier_semaphore()
    partners = [sibling, *y_to.values(), *z_to.values(), *x_to.values()]
    for partner in partners:
        pl.semaphore_signal(barrier, inc=1, device_id=partner, device_id_type=MESH)
    pl.semaphore_wait(barrier, len(partners))

    def y_at(d):
        return lax.rem(y + d + 2 * NY, NY)

    def z_at(d):
        return lax.rem(z + d + 2 * NZ, NZ)

    def far_half(d, far):
        return 0 if (d == 1) == far else 1

    zx, xz = pl.ds(0, ZX), pl.ds(ZX, CH - ZX)
    h_x = {d: send(g_in.at[:, xz], G.at[z, x, :, xz], to) for d, to in x_to.items()}
    g_z = {d: send(g_in.at[:, zx], G.at[z, x, :, zx], to) for d, to in z_to.items()}
    g_x = {(d, 0): send(g_in.at[:, zx], G.at[z, x, :, zx], to) for d, to in x_to.items()}
    s_y = {}
    for far in (True, False):
        for d in (1, -1):
            h = far_half(d, far)
            s_y[d, h, 0] = send(s_in.at[h], S.at[y * 2 + core, h], y_to[d])
    s_sib = [send(s_in, S.at[y * 2 + core], sibling)]
    codes = send(c_in, W.at[1], sibling)

    def forward_g(d):
        g_z[d].wait_recv()
        chunk = G.at[z_at(-d), x, :, zx]
        for dx, to in x_to.items():
            g_x[dx, d] = send(chunk, chunk, to)

    def forward_s(step, far):
        for d in (1, -1):
            h = far_half(d, far)
            s_y[d, h, step].wait_recv()
            block = S.at[y_at(-d * (step + 1)) * 2 + core, h]
            if step < (3 if far else 2):
                s_y[d, h, step + 1] = send(block, block, y_to[d])
            s_sib.append(send(block, block, sibling))

    own_e.wait()
    scale = jnp.exp2((E[...] + 14).astype(jnp.float32)).astype(jnp.bfloat16).reshape(1, 1, CH)
    own_g.wait()
    for d in (1, -1):
        forward_g(d)
    for d in x_to:
        h_x[d].wait_recv()
    h_z = {d: send(G.at[z, :, :, xz], G.at[z, :, :, xz], to) for d, to in z_to.items()}
    for d in (2, -2):
        forward_g(d)
    forward_s(0, True)
    for d in (3, -3):
        forward_g(d)
    forward_s(0, False)
    forward_g(4)

    def arrived(d):
        for dx in x_to:
            g_x[dx, d].wait_recv()
        if d:
            h_z[d].wait_recv()

    for d in (0, 1, -1, 2, -2):
        arrived(d)
    forward_s(1, True)
    for d in (3, -3):
        arrived(d)
    forward_s(1, False)
    arrived(4)
    def scaled(slots, part, out):
        for k in slots:
            block = G[y_at(ORDER[k]), pl.ds(2 * part, 2)] * scale
            out[k] = block.reshape(TB, CH)

    first, second, rest = range(0, 1), range(1, 3), range(3, NY)
    acts = {}

    def exchange(slots):
        at = pl.ds(slots[0], len(slots))
        scaled(slots, 1 - core, T)
        acts[slots] = send(T.at[at], A.at[1, at], sibling)
        scaled(slots, core, A.at[0])

    def matmul(slots):
        at, rows = pl.ds(slots[0], len(slots)), len(slots) * TB

        def tile(cols):
            return sum(
                jnp.dot(A[i, at].reshape(rows, CH), W[i, :, cols], preferred_element_type=jnp.float32) for i in (0, 1)
            )

        @pl.loop(0, LANES // 2)
        def _(j):
            value = tile(pl.ds(pl.multiple_of(j * 256, 256), 256))
            for i in (0, 1):
                Q[at, :, j * 2 + i] = value[:, i * 128 : i * 128 + 128].reshape(len(slots), 4, 16, 128)

        Q[at, :, LANES - 1] = tile(pl.ds(128 * (LANES - 1), 128)).reshape(len(slots), 4, 16, 128)

    sums = {}

    def chains(step, longer):
        starts = 0 if longer else 1
        for g in (0, 1):
            for k, d in enumerate((1, -1)):
                h = k if longer else 1 - k
                value = Q[ORDER.index(d * (4 - step) if step else 4), 2 * h + g]
                if step > starts:
                    sums[k, h, g, step - 1].wait_recv()
                    value += decode(RX.at[k, h, g, step - 1])
                out = TX.at[k, h, g, step]
                encode(value, out)
                sums[k, h, g, step] = send(out, RX.at[k, h, g, step], y_to[d])

    def finish():
        for h in (0, 1):
            for g in (0, 1):
                value = Q[NY - 1, 2 * h + g]
                for k in (0, 1):
                    sums[k, h, g, 3].wait_recv()
                    value += decode(RX.at[k, h, g, 3])
                value = (value * 2.0**-14).astype(jnp.bfloat16)
                for j in range(LANES):
                    ig_out[pl.ds(32 * h + 16 * g, 16), pl.ds(128 * j, 128)] = value[j]

    def wgrad():
        def tile(cols, width):
            value = jnp.dot(GT[...], S[:, :, :, cols].reshape(1024, width), preferred_element_type=jnp.float32)
            WG[:, cols] = value.astype(jnp.bfloat16)

        @pl.loop(0, LANES // 2)
        def _(j):
            tile(pl.ds(pl.multiple_of(j * 256, 256), 256), 256)

        tile(pl.ds(128 * (LANES - 1), 128), 128)
        return local(WG, wg_out, 4)

    exchange(first)
    exchange(second)
    own_c.wait()
    codes.wait_recv()
    acts[first].wait_recv()
    matmul(first)
    chains(0, True)
    acts[second].wait_recv()
    matmul(second)
    chains(1, False)
    exchange(rest)
    forward_s(2, True)
    acts[rest].wait_recv()
    matmul(rest)
    GT[...] = G[...].reshape(1024, CH).T
    chains(1, True)
    chains(2, False)
    forward_s(2, False)
    chains(2, True)
    chains(3, False)
    chains(3, True)
    forward_s(3, True)
    own_s.wait()
    for copy in s_sib:
        copy.wait_recv()
    ends = [wgrad()]
    finish()
    for copy in ends:
        copy.wait()
    for copy in sent:
        copy.wait_send()


def store(ig_in, wg_in, ig_out, wg_out, sem):
    copies = [pltpu.make_async_copy(wg_in, wg_out, sem.at[0]), pltpu.make_async_copy(ig_in, ig_out, sem.at[1])]
    for copy in copies:
        copy.start()
    for copy in copies:
        copy.wait()


def local_part(grad_out, saved_input, codes, exponents):
    any_, hbm = pl.BlockSpec(memory_space=pl.ANY), pl.BlockSpec(memory_space=pltpu.HBM)
    bf16 = jnp.bfloat16
    message = (2, 2, 2, 4, LANES + 1, 16, 128)
    shapes = (jax.ShapeDtypeStruct((TB, FB), bf16), jax.ShapeDtypeStruct((CH, FB), bf16))
    grads = pl.pallas_call(
        kernel,
        out_shape=shapes,
        in_specs=[hbm, hbm, hbm, hbm],
        out_specs=(pl.BlockSpec(memory_space=pltpu.VMEM), any_),
        scratch_shapes=[
            pltpu.VMEM((2 * NY, 2, 32, FB), bf16),
            pltpu.VMEM((NZ, NX, 32, CH), bf16),
            pltpu.VMEM((2, CH, FB), bf16),
            pltpu.VMEM((CH,), jnp.int32),
            pltpu.VMEM((2, NY, TB, CH), bf16),
            pltpu.VMEM((NY, TB, CH), bf16),
            pltpu.VMEM((CH, 2 * NY * TB), bf16),
            pltpu.VMEM((NY, 4, LANES, 16, 128), jnp.float32),
            pltpu.VMEM((CH, FB), bf16),
            pltpu.VMEM(message, jnp.int16),
            pltpu.VMEM(message, jnp.int16),
            pltpu.SemaphoreType.DMA((5,)),
            pltpu.SemaphoreType.DMA((COPIES,)),
            pltpu.SemaphoreType.DMA((COPIES,)),
        ],
        compiler_params=pltpu.CompilerParams(collective_id=0, has_side_effects=True, vmem_limit_bytes=VMEM_LIMIT),
        cost_estimate=pl.CostEstimate(flops=4 * 1024 * CH * FB, bytes_accessed=8_000_000, transcendentals=0),
    )(*(pltpu.with_memory_space_constraint(a, pltpu.HBM) for a in (grad_out, saved_input.reshape(2, 32, FB), codes, exponents)))
    return pl.pallas_call(
        store,
        out_shape=shapes,
        in_specs=[any_, any_],
        out_specs=(any_, any_),
        scratch_shapes=[pltpu.SemaphoreType.DMA((2,))],
        compiler_params=pltpu.CompilerParams(vmem_limit_bytes=1024 * 1024),
    )(*grads)


def solution(mesh):
    in_specs = (P("col", "row"), P("row", "col"), P("row", "col"), P("row"))
    out_specs = (P("row", "col"), P("row", "col"))
    return jax.shard_map(local_part, mesh=mesh, in_specs=in_specs, out_specs=out_specs, check_vma=False)
```

```python
import jax
import jax.numpy as jnp
from jax import lax
from jax.experimental import pallas as pl
from jax.experimental.pallas import tpu as pltpu
from jax.sharding import PartitionSpec as P

MESH = pl.DeviceIdType.MESH
NY, NZ, NX = 8, 8, 4
CH, FB, TB = 512, 1664, 64
LANES = FB // 128
TOP = 32700.0
COPIES = 112
ZX = 384
ORDER = (4, 3, -3, 2, -2, 1, -1, 0)
VMEM_LIMIT = 52 * 1000 * 1024


def encode(value, out):
    top = jnp.max(jnp.max(jnp.abs(value), axis=0), axis=1, keepdims=True)
    code = jnp.ceil(16.0 * jnp.log2(jnp.maximum(top, 1e-30)))
    scale = jnp.exp2(code * (-1.0 / 16)) * TOP
    out[pl.ds(0, LANES)] = jnp.round(value * scale[None]).astype(jnp.int32).astype(jnp.int16)
    out[LANES] = jnp.broadcast_to(code, (16, 128)).astype(jnp.int32).astype(jnp.int16)


def decode(message):
    scale = jnp.exp2(message[LANES].astype(jnp.int32).astype(jnp.float32) * (1.0 / 16)) * (1.0 / TOP)
    return message[pl.ds(0, LANES)].astype(jnp.int32).astype(jnp.float32) * scale[None]


def kernel(g_in, s_in, c_in, e_in, ig_out, wg_out, S, G, W, E, A, T, GT, Q, WG, TX, RX, lsem, ssem, rsem):
    row, col = lax.axis_index("row"), lax.axis_index("col")
    y, core = lax.div(row, 2), lax.rem(row, 2)
    z, x = lax.div(col, NX), lax.rem(col, NX)
    sent = []

    def device(dy=0, dz=0, dx=0, other=False):
        yy = lax.rem(y + dy + NY, NY)
        cc = 1 - core if other else core
        return (yy * 2 + cc, lax.rem(z + dz + NZ, NZ) * NX + lax.rem(x + dx + NX, NX))

    def send(src, dst, to):
        k = len(sent)
        copy = pltpu.make_async_remote_copy(
            src_ref=src, dst_ref=dst, send_sem=ssem.at[k], recv_sem=rsem.at[k], device_id=to, device_id_type=MESH
        )
        copy.start()
        sent.append(copy)
        return copy

    def local(src, dst, k):
        copy = pltpu.make_async_copy(src, dst, lsem.at[k])
        copy.start()
        return copy

    sibling = device(other=True)
    y_to = {d: device(dy=d) for d in (1, -1)}
    z_to = {d: device(dz=d) for d in (1, -1, 2, -2, 3, -3, 4)}
    x_to = {d: device(dx=d) for d in (2, 1, -1)}

    own_g = local(g_in, G.at[z, x], 0)
    own_s = local(s_in, S.at[y * 2 + core], 1)
    own_c = local(c_in, W.at[0], 2)
    own_e = local(e_in, E, 3)

    barrier = pltpu.get_barrier_semaphore()
    partners = [sibling, *y_to.values(), *z_to.values(), *x_to.values()]
    for partner in partners:
        pl.semaphore_signal(barrier, inc=1, device_id=partner, device_id_type=MESH)
    pl.semaphore_wait(barrier, len(partners))

    def y_at(d):
        return lax.rem(y + d + 2 * NY, NY)

    def z_at(d):
        return lax.rem(z + d + 2 * NZ, NZ)

    def far_half(d, far):
        return 0 if (d == 1) == far else 1

    zx, xz = pl.ds(0, ZX), pl.ds(ZX, CH - ZX)
    h_x = {d: send(g_in.at[:, xz], G.at[z, x, :, xz], to) for d, to in x_to.items()}
    g_z = {d: send(g_in.at[:, zx], G.at[z, x, :, zx], to) for d, to in z_to.items()}
    g_x = {(d, 0): send(g_in.at[:, zx], G.at[z, x, :, zx], to) for d, to in x_to.items()}
    s_y = {}
    for far in (True, False):
        for d in (1, -1):
            h = far_half(d, far)
            s_y[d, h, 0] = send(s_in.at[h], S.at[y * 2 + core, h], y_to[d])
    s_sib = [send(s_in, S.at[y * 2 + core], sibling)]
    codes = send(c_in, W.at[1], sibling)

    def forward_g(d):
        g_z[d].wait_recv()
        chunk = G.at[z_at(-d), x, :, zx]
        for dx, to in x_to.items():
            g_x[dx, d] = send(chunk, chunk, to)

    def forward_s(step, far):
        for d in (1, -1):
            h = far_half(d, far)
            s_y[d, h, step].wait_recv()
            block = S.at[y_at(-d * (step + 1)) * 2 + core, h]
            if step < (3 if far else 2):
                s_y[d, h, step + 1] = send(block, block, y_to[d])
            s_sib.append(send(block, block, sibling))

    own_e.wait()
    scale = jnp.exp2((E[...] + 14).astype(jnp.float32)).astype(jnp.bfloat16).reshape(1, 1, CH)
    own_g.wait()
    for d in (1, -1):
        forward_g(d)
    for d in x_to:
        h_x[d].wait_recv()
    h_z = {d: send(G.at[z, :, :, xz], G.at[z, :, :, xz], to) for d, to in z_to.items()}
    forward_s(0, True)
    for d in (2, -2):
        forward_g(d)
    for d in (3, -3):
        forward_g(d)
    forward_s(0, False)
    forward_g(4)

    def arrived(d):
        for dx in x_to:
            g_x[dx, d].wait_recv()
        if d:
            h_z[d].wait_recv()

    for d in (0, 1, -1, 2, -2):
        arrived(d)
    forward_s(1, True)
    for d in (3, -3):
        arrived(d)
    forward_s(1, False)
    arrived(4)
    def scaled(slots, part, out):
        for k in slots:
            block = G[y_at(ORDER[k]), pl.ds(2 * part, 2)] * scale
            out[k] = block.reshape(TB, CH)

    first, second, rest = range(0, 1), range(1, 3), range(3, NY)
    acts = {}

    def exchange(slots):
        at = pl.ds(slots[0], len(slots))
        scaled(slots, 1 - core, T)
        acts[slots] = send(T.at[at], A.at[1, at], sibling)
        scaled(slots, core, A.at[0])

    def matmul(slots):
        at, rows = pl.ds(slots[0], len(slots)), len(slots) * TB

        def tile(cols):
            return sum(
                jnp.dot(A[i, at].reshape(rows, CH), W[i, :, cols], preferred_element_type=jnp.float32) for i in (0, 1)
            )

        @pl.loop(0, LANES // 2)
        def _(j):
            value = tile(pl.ds(pl.multiple_of(j * 256, 256), 256))
            for i in (0, 1):
                Q[at, :, j * 2 + i] = value[:, i * 128 : i * 128 + 128].reshape(len(slots), 4, 16, 128)

        Q[at, :, LANES - 1] = tile(pl.ds(128 * (LANES - 1), 128)).reshape(len(slots), 4, 16, 128)

    sums = {}

    def chains(step, longer):
        starts = 0 if longer else 1
        for g in (0, 1):
            for k, d in enumerate((1, -1)):
                h = k if longer else 1 - k
                value = Q[ORDER.index(d * (4 - step) if step else 4), 2 * h + g]
                if step > starts:
                    sums[k, h, g, step - 1].wait_recv()
                    value += decode(RX.at[k, h, g, step - 1])
                out = TX.at[k, h, g, step]
                encode(value, out)
                sums[k, h, g, step] = send(out, RX.at[k, h, g, step], y_to[d])

    def finish():
        for h in (0, 1):
            for g in (0, 1):
                value = Q[NY - 1, 2 * h + g]
                for k in (0, 1):
                    sums[k, h, g, 3].wait_recv()
                    value += decode(RX.at[k, h, g, 3])
                value = (value * 2.0**-14).astype(jnp.bfloat16)
                for j in range(LANES):
                    ig_out[pl.ds(32 * h + 16 * g, 16), pl.ds(128 * j, 128)] = value[j]

    def wgrad():
        def tile(cols, width):
            value = jnp.dot(GT[...], S[:, :, :, cols].reshape(1024, width), preferred_element_type=jnp.float32)
            WG[:, cols] = value.astype(jnp.bfloat16)

        @pl.loop(0, LANES // 2)
        def _(j):
            tile(pl.ds(pl.multiple_of(j * 256, 256), 256), 256)

        tile(pl.ds(128 * (LANES - 1), 128), 128)
        return local(WG, wg_out, 4)

    exchange(first)
    exchange(second)
    own_c.wait()
    codes.wait_recv()
    acts[first].wait_recv()
    matmul(first)
    chains(0, True)
    acts[second].wait_recv()
    matmul(second)
    chains(1, False)
    exchange(rest)
    forward_s(2, True)
    acts[rest].wait_recv()
    matmul(rest)
    GT[...] = G[...].reshape(1024, CH).T
    chains(1, True)
    chains(2, False)
    forward_s(2, False)
    chains(2, True)
    chains(3, False)
    chains(3, True)
    forward_s(3, True)
    own_s.wait()
    for copy in s_sib:
        copy.wait_recv()
    ends = [wgrad()]
    finish()
    for copy in ends:
        copy.wait()
    for copy in sent:
        copy.wait_send()


def store(ig_in, wg_in, ig_out, wg_out, sem):
    copies = [pltpu.make_async_copy(wg_in, wg_out, sem.at[0]), pltpu.make_async_copy(ig_in, ig_out, sem.at[1])]
    for copy in copies:
        copy.start()
    for copy in copies:
        copy.wait()


def local_part(grad_out, saved_input, codes, exponents):
    any_, hbm = pl.BlockSpec(memory_space=pl.ANY), pl.BlockSpec(memory_space=pltpu.HBM)
    bf16 = jnp.bfloat16
    message = (2, 2, 2, 4, LANES + 1, 16, 128)
    shapes = (jax.ShapeDtypeStruct((TB, FB), bf16), jax.ShapeDtypeStruct((CH, FB), bf16))
    grads = pl.pallas_call(
        kernel,
        out_shape=shapes,
        in_specs=[hbm, hbm, hbm, hbm],
        out_specs=(pl.BlockSpec(memory_space=pltpu.VMEM), any_),
        scratch_shapes=[
            pltpu.VMEM((2 * NY, 2, 32, FB), bf16),
            pltpu.VMEM((NZ, NX, 32, CH), bf16),
            pltpu.VMEM((2, CH, FB), bf16),
            pltpu.VMEM((CH,), jnp.int32),
            pltpu.VMEM((2, NY, TB, CH), bf16),
            pltpu.VMEM((NY, TB, CH), bf16),
            pltpu.VMEM((CH, 2 * NY * TB), bf16),
            pltpu.VMEM((NY, 4, LANES, 16, 128), jnp.float32),
            pltpu.VMEM((CH, FB), bf16),
            pltpu.VMEM(message, jnp.int16),
            pltpu.VMEM(message, jnp.int16),
            pltpu.SemaphoreType.DMA((5,)),
            pltpu.SemaphoreType.DMA((COPIES,)),
            pltpu.SemaphoreType.DMA((COPIES,)),
        ],
        compiler_params=pltpu.CompilerParams(collective_id=0, has_side_effects=True, vmem_limit_bytes=VMEM_LIMIT),
        cost_estimate=pl.CostEstimate(flops=4 * 1024 * CH * FB, bytes_accessed=8_000_000, transcendentals=0),
    )(*(pltpu.with_memory_space_constraint(a, pltpu.HBM) for a in (grad_out, saved_input.reshape(2, 32, FB), codes, exponents)))
    return pl.pallas_call(
        store,
        out_shape=shapes,
        in_specs=[any_, any_],
        out_specs=(any_, any_),
        scratch_shapes=[pltpu.SemaphoreType.DMA((2,))],
        compiler_params=pltpu.CompilerParams(vmem_limit_bytes=1024 * 1024),
    )(*grads)


def solution(mesh):
    in_specs = (P("col", "row"), P("row", "col"), P("row", "col"), P("row"))
    out_specs = (P("row", "col"), P("row", "col"))
    return jax.shard_map(local_part, mesh=mesh, in_specs=in_specs, out_specs=out_specs, check_vma=False)
```
